32 devices in a mesh: freq: 8 (over z, x), rec: 4 (over y, core).
Axes of the slice: x: 2, y: 2, z: 4, core: 2. Of those that a mesh axis runs over, the one named last changes fastest.
Arguments:
- response: float32 [2, 128, 1024, 1024], P(None, 'freq', 'rec'), may hold values from -0.1875 to 0.1875
- focus_plus: float32 [2, 128, 1024, 64], P(None, 'freq', 'rec'), may hold values from -6 to 6
- direct: float32 [2, 128, 1024, 64], P(None, 'freq', 'rec'), may hold values from -6 to 6
- onset: int32 [1024, 64], P('rec'), may hold values from 4 to 64
Outputs:
- focus_minus: float32 [2, 128, 1024, 64], P(None, 'freq', 'rec')
- focus_plus_next: float32 [2, 128, 1024, 64], P(None, 'freq', 'rec')
The draws below stay inside these ranges and needn't reach their ends.
All inputs are finite; a program needn't handle non-finite values.
Results may differ from the reference program's by a relative error of at most 0.00007.
Values sent between devices are 32-bit elements; how exact they have to be, the bound alone decides.
A program may use at most 192 MiB of HBM per device.

```python
import jax
import jax.numpy as jnp
from jax import lax

N = 1024
NF = 128
FOCAL = 64


def set_ends(drawn, key, least, largest):
    longest = drawn.shape.index(max(drawn.shape))
    spots = []
    for shift in (0, 1):
        where = [jax.random.randint(jax.random.fold_in(key, axis), (), 0, length) for axis, length in enumerate(drawn.shape)]
        where[longest] = (where[longest] + shift) % drawn.shape[longest]
        spots.append(tuple(where))
    return drawn.at[spots[0]].set(least).at[spots[1]].set(largest)


def levels(rng, extent, cuts, low, top_value):
    loudness = 1.0
    for axis_at, parts in cuts:
        heights = jax.random.uniform(jax.random.fold_in(jax.random.fold_in(rng, 6), axis_at), (parts,), jnp.float32, low / len(cuts), top_value / len(cuts))
        loudness = loudness * jnp.repeat(jnp.exp(heights), extent[axis_at] // parts).reshape((-1,) + (1,) * (len(extent) - 1 - axis_at))
    return loudness


def normal_values(rng, dims, scale, reach, pieces=(), kind=jnp.bfloat16):
    array = jax.random.normal(rng, dims, jnp.float32) * scale
    if len(pieces) > 0:
        array = levels(rng, dims, pieces, -0.22, 0.18) * array
    return jnp.clip(array, min=-reach, max=reach).astype(kind)


def setup_inputs(seed: int = 0) -> dict:
    key_of = jax.random.split(jax.random.key(seed), 5)
    return {
        "response": normal_values(key_of[0], (2, NF, N, N), N ** -0.5, 0.1875, ((1, 8), (2, 4)), jnp.float32),
        "focus_plus": normal_values(key_of[1], (2, NF, N, FOCAL), 1.0, 6.0, ((1, 8), (2, 4)), jnp.float32),
        "direct": normal_values(key_of[2], (2, NF, N, FOCAL), 1.0, 6.0, ((1, 8), (2, 4)), jnp.float32),
        "onset": set_ends(jax.random.randint(key_of[3], (N, FOCAL), 4, NF // 2 + 1), jax.random.fold_in(key_of[3], 1), 4, (NF // 2 + 1) - 1).astype(jnp.int32),
    }


def full_dot(left, right):
    return jnp.dot(left, right, precision=lax.Precision.HIGHEST)


def reference(response, focus_plus, direct, onset):
    counter = jnp.arange(NF, dtype=jnp.int32)
    distance = jnp.minimum(counter, NF - counter)
    window_mask = distance[:, None, None] < onset[None, :, :]

    def apply_window(real_part, imag_part):
        spectra = real_part + 1j * imag_part
        in_time = jnp.fft.ifft(spectra, axis=0)
        in_time = jnp.where(window_mask, in_time, 0.0)
        result = jnp.fft.fft(in_time, axis=0)
        return jnp.real(result), jnp.imag(result)

    def forward_one(inputs):
        real_block, imag_block, plus_real, plus_imag = inputs
        return (full_dot(real_block, plus_real) - full_dot(imag_block, plus_imag),
                full_dot(real_block, plus_imag) + full_dot(imag_block, plus_real))

    g_real, g_imag = lax.map(forward_one, (response[0], response[1], focus_plus[0], focus_plus[1]))
    minus_real, minus_imag = apply_window(g_real, g_imag)

    def adjoint_one(inputs):
        real_block, imag_block, minus_re, minus_im = inputs
        return (full_dot(real_block.T, minus_re) + full_dot(imag_block.T, minus_im),
                full_dot(real_block.T, minus_im) - full_dot(imag_block.T, minus_re))

    h_real, h_imag = lax.map(adjoint_one, (response[0], response[1], minus_real, minus_imag))
    upd_real, upd_imag = apply_window(h_real, h_imag)
    focus_minus = jnp.stack([minus_real, minus_imag])
    focus_plus_next = direct + jnp.stack([upd_real, upd_imag])
    return focus_minus, focus_plus_next
```

```python
import functools
import math

import jax
import jax.numpy as jnp
import ml_dtypes
import numpy as np
from jax import lax
from jax.experimental import pallas as pl
from jax.experimental.pallas import tpu as pltpu
from jax.sharding import PartitionSpec as P

MESH = pl.DeviceIdType.MESH
SLOTS = 4
TILE = 8


def full_einsum(form, left, right):
    return jnp.einsum(form, left, right, precision=lax.Precision.HIGHEST)


def make_tables(freq_total):
    counter = jnp.arange(freq_total, dtype=jnp.int32)
    phase_steps = counter[:, None] * counter[None, :] % freq_total
    phase_angle = phase_steps.astype(jnp.float32) * (2.0 * math.pi / freq_total)
    cosine = jnp.cos(phase_angle)
    sine_table = jnp.sin(phase_angle)
    inverse = (
        jnp.concatenate(
            [jnp.concatenate([cosine, -sine_table], 1), jnp.concatenate([sine_table, cosine], 1)], 0
        )
        / freq_total
    )
    forward = jnp.concatenate(
        [jnp.concatenate([cosine, sine_table], 1), jnp.concatenate([-sine_table, cosine], 1)], 0
    )
    return (inverse, forward)


def windowed(traces, onset_flat, inverse, forward):
    freq_total = traces.shape[1]
    stacked = traces.reshape(2 * freq_total, -1)
    time_traces = jnp.dot(inverse, stacked, precision=lax.Precision.HIGHEST)
    counter = jnp.arange(freq_total, dtype=jnp.int32)
    distance = jnp.minimum(counter, freq_total - counter)
    window_mask = (distance[:, None] < onset_flat[None, :]).astype(jnp.float32)
    window_mask = jnp.concatenate([window_mask, window_mask], 0)
    spectra = jnp.dot(forward, time_traces * window_mask, precision=lax.Precision.HIGHEST)
    return spectra.reshape(traces.shape)


def per_device_general(response, focus_plus, direct, onset):
    freq_dev = response.shape[1]
    row_count = response.shape[2]
    focal_count = focus_plus.shape[3]
    groups = lax.axis_size("freq")
    freq_index = lax.axis_index("freq")
    flat_count = row_count * focal_count
    piece_len = flat_count // groups
    local_onset = lax.dynamic_slice_in_dim(onset.reshape(-1), freq_index * piece_len, piece_len, 0)
    inverse, forward = make_tables(freq_dev * groups)
    shard_piece = lax.all_gather(focus_plus, "rec", axis=2, tiled=True)
    joined = jnp.concatenate([shard_piece[0], shard_piece[1]], axis=2)
    from_real = full_einsum("wrs,wsf->wrf", response[0], joined)
    from_imag = full_einsum("wrs,wsf->wrf", response[1], joined)
    new_real = from_real[:, :, :focal_count] - from_imag[:, :, focal_count:]
    new_imag = from_real[:, :, focal_count:] + from_imag[:, :, :focal_count]
    spectra = jnp.stack([new_real, new_imag]).reshape(2, freq_dev, flat_count)
    in_time = lax.all_to_all(spectra, "freq", split_axis=2, concat_axis=1, tiled=True)
    filtered = windowed(in_time, local_onset, inverse, forward)
    focus_minus = lax.all_to_all(filtered, "freq", split_axis=1, concat_axis=2, tiled=True).reshape(
        2, freq_dev, row_count, focal_count
    )
    minus_joined = jnp.concatenate([focus_minus[0], focus_minus[1]], axis=2)
    from_real = full_einsum("wrs,wrf->swf", response[0], minus_joined)
    from_imag = full_einsum("wrs,wrf->swf", response[1], minus_joined)
    h_real = from_real[:, :, :focal_count] + from_imag[:, :, focal_count:]
    h_imag = from_real[:, :, focal_count:] - from_imag[:, :, :focal_count]
    summed = lax.psum_scatter(
        jnp.stack([h_real, h_imag], axis=1), "rec", scatter_dimension=0, tiled=True
    )
    arranged_sum = jnp.transpose(summed, (1, 2, 0, 3)).reshape(2, freq_dev, flat_count)
    arranged = lax.all_to_all(arranged_sum, "freq", split_axis=2, concat_axis=1, tiled=True)
    windowed_back = windowed(arranged, local_onset, inverse, forward)
    returned = lax.all_to_all(
        windowed_back, "freq", split_axis=1, concat_axis=2, tiled=True
    ).reshape(2, freq_dev, row_count, focal_count)
    return (focus_minus, direct + returned)


def cas_tables(groups):
    total = 2 * TILE * groups
    order = np.array(
        [g * 2 * TILE + half * TILE + k for half in range(2) for g in range(groups) for k in range(TILE)]
    )
    step = np.arange(total)[:, None] * order[None, :] % total
    angle = step * (2.0 * math.pi / total)
    into = np.cos(angle) + np.sin(angle)

    def table(matrix):
        hi = matrix.astype(ml_dtypes.bfloat16)
        lo = (matrix - hi.astype(np.float64)).astype(ml_dtypes.bfloat16)
        return np.concatenate(
            [np.concatenate([hi, hi], 1), np.concatenate([lo, np.zeros_like(lo)], 1)], 0
        )

    return table(into), table(into.T / total)


def split(value):
    hi = value.astype(jnp.bfloat16)
    lo = (value - hi.astype(jnp.float32)).astype(jnp.bfloat16)
    return hi, lo


def dot(left, right, left_dim, right_dim):
    return lax.dot_general(
        left, right, (((left_dim,), (right_dim,)), ((), ())), preferred_element_type=jnp.float32
    )


def kernel(
    groups,
    resp, plus, direct, onset, into, back,
    minus_out, next_out,
    gathered, rbuf, g_buf, x1, y_buf, fm, part, core_in, y_in, x2, upd,
    ag_s, ag_r, own_sem, r_sem, a_s, a_r, rc_s, rc_r, ry_s, ry_r,
):
    me = lax.axis_index("freq")
    rec = lax.axis_index("rec")
    core = lax.rem(rec, 2)
    sibling = rec + 1 - 2 * core
    across = lax.rem(rec + 2, 4)
    diagonal = lax.rem(sibling + 2, 4)
    rows = resp.shape[2]
    lane_parts = rows // 128
    focal = plus.shape[2]
    total = 2 * TILE * groups

    barrier = pltpu.get_barrier_semaphore()
    for d in range(1, groups):
        pl.semaphore_signal(
            barrier, inc=1, device_id=(lax.rem(me + d, groups), rec), device_id_type=MESH
        )
    for other in (sibling, across):
        pl.semaphore_signal(barrier, inc=1, device_id=(me, other), device_id_type=MESH)

    def response_copy(w, slot):
        return pltpu.make_async_copy(resp.at[:, w], rbuf.at[slot], r_sem.at[slot])

    for k in range(SLOTS):
        response_copy(k, k).start()
    pl.semaphore_wait(barrier, groups + 1)

    def remote(src, dst, s_sem, d_sem, to):
        return pltpu.make_async_remote_copy(
            src_ref=src, dst_ref=dst, send_sem=s_sem, recv_sem=d_sem, device_id=to, device_id_type=MESH
        )

    def ag_copy(kind, half):
        span = pl.ds(half * TILE, TILE)
        if kind == 2:
            return remote(
                gathered.at[across, :, span], gathered.at[across, :, span],
                ag_s.at[2, half], ag_r.at[2, half], (me, sibling),
            )
        return remote(
            plus.at[:, span], gathered.at[rec, :, span],
            ag_s.at[kind, half], ag_r.at[kind, half], (me, (across, sibling)[kind]),
        )

    def ag_landed(kind, half):
        span = pl.ds(half * TILE, TILE)
        slot = (across, sibling, diagonal)[kind]
        place = gathered.at[slot, :, span]
        return remote(
            place, place, ag_s.at[kind, half], ag_r.at[kind, half], (me, (across, sibling, sibling)[kind])
        )

    def a2a_copies(phase, half, src, dst):
        return [
            remote(
                src.at[half, :, :, peer], dst.at[half, :, :, me],
                a_s.at[phase, d], a_r.at[phase, d], (peer, rec),
            )
            for d in range(1, groups)
            for peer in (lax.rem(me + d, groups),)
        ]

    def a2a_own(phase, half, src, dst):
        return pltpu.make_async_copy(src.at[half, :, :, me], dst.at[half, :, :, me], a_r.at[phase, 0])

    def a2a_start(phase, half, src, dst):
        for copy in a2a_copies(phase, half, src, dst):
            copy.start()
        a2a_own(phase, half, src, dst).start()

    def a2a_sent(phase, half, src, dst):
        for copy in a2a_copies(phase, half, src, dst):
            copy.wait_send()

    def a2a_landed(phase, half, src, dst):
        a2a_own(phase, half, src, dst).wait()
        for d in range(1, groups):
            peer = lax.rem(me + groups - d, groups)
            place = dst.at[half, :, :, peer]
            remote(place, place, a_s.at[phase, d], a_r.at[phase, d], (peer, rec)).wait_recv()

    def spread(dst, half, k, value):
        for lh in range(lane_parts):
            for c in range(2):
                for grp in range(groups):
                    at = (c * groups + grp) * TILE
                    dst[half, lh, c, grp, pl.ds(k, TILE, stride=TILE), :] = value[
                        at : at + TILE, lh * 128 : (lh + 1) * 128
                    ]

    def window(src, dst):
        time = lax.broadcasted_iota(jnp.int32, (total, rows), 0)
        distance = jnp.minimum(time, total - time)

        def one(f, carry):
            span = pl.ds(pl.multiple_of(f * TILE, TILE), TILE)
            keep = distance < onset[me, pl.ds(f, 1), :]
            for c in range(2):
                block = jnp.concatenate(
                    [
                        jnp.concatenate(
                            [src[half, lh, c, :, span, :].reshape(groups * TILE, 128) for half in range(2)], 0
                        )
                        for lh in range(lane_parts)
                    ],
                    1,
                )
                for step in range(2):
                    hi, lo = split(block)
                    both = dot((into, back)[step][...], jnp.concatenate([hi, lo], 0), 1, 0)
                    block = both[:total] + both[total:]
                    if step == 0:
                        block = jnp.where(keep, block, 0.0)
                for half in range(2):
                    for lh in range(lane_parts):
                        dst[half, lh, c, :, span, :] = block[
                            half * groups * TILE : (half + 1) * groups * TILE, lh * 128 : (lh + 1) * 128
                        ].reshape(groups, TILE, 128)
            return carry

        lax.fori_loop(0, TILE, one, 0)

    own = pltpu.make_async_copy(plus, gathered.at[rec], own_sem)
    own.start()
    ag_copy(0, 0).start()
    ag_copy(1, 0).start()
    ag_copy(1, 1).start()
    own.wait()

    def g_step(half, k, carry):
        w = half * TILE + k
        slot = lax.rem(k, SLOTS)
        response_copy(w, slot).wait()
        plus_t = jnp.concatenate(
            [jnp.concatenate([gathered[q, c, w] for q in range(4)], 1) for c in range(2)], 0
        )
        f_hi, f_lo = split(plus_t)
        f_both = jnp.concatenate([f_hi, f_lo], 0)
        products = []
        for c in range(2):
            hi, lo = split(rbuf[slot, c])
            wide = dot(hi, f_both, 1, 1)
            products.append(wide[:, : 2 * focal] + wide[:, 2 * focal :] + dot(lo, f_hi, 1, 1))
        p_t, q_t = products[0].T, products[1].T
        spread(g_buf, half, k, jnp.concatenate([p_t[:focal] - q_t[focal:], p_t[focal:] + q_t[:focal]], 0))
        response_copy(lax.rem(w + SLOTS, 2 * TILE), slot).start()
        return carry

    for half in range(2):
        ag_landed(0, half).wait_recv()
        if half == 0:
            ag_copy(0, 0).wait_send()
            ag_copy(0, 1).start()
        ag_copy(2, half).start()
        ag_landed(1, half).wait_recv()
        ag_landed(2, half).wait_recv()
        lax.fori_loop(0, TILE, functools.partial(g_step, half), 0)
        a2a_start(half, half, g_buf, x1)
    for half in range(2):
        a2a_landed(half, half, g_buf, x1)

    window(x1, y_buf)

    a2a_start(2, 0, y_buf, fm)
    a2a_sent(2, 0, y_buf, fm)
    a2a_start(3, 1, y_buf, fm)

    def core_copy(half, yy):
        return remote(
            part.at[half, 2 * yy + 1 - core], core_in.at[half, yy],
            rc_s.at[half, yy], rc_r.at[half, yy], (me, sibling),
        )

    def y_copy(half):
        return remote(
            part.at[half, across], y_in.at[half], ry_s.at[half], ry_r.at[half], (me, across)
        )

    def collect(src, half, k):
        return jnp.concatenate(
            [
                jnp.concatenate(
                    [
                        src[half, lh, c, grp, pl.ds(k, TILE, stride=TILE), :]
                        for c in range(2)
                        for grp in range(groups)
                    ],
                    0,
                )
                for lh in range(lane_parts)
            ],
            1,
        )

    def h_step(half, k, carry):
        w = half * TILE + k
        slot = lax.rem(k, SLOTS)
        minus_t = collect(fm, half, k)
        for c in range(2):
            minus_out[c, w] = minus_t[c * focal : (c + 1) * focal]
        response_copy(w, slot).wait()
        m_hi, m_lo = split(minus_t)
        m_both = jnp.concatenate([m_hi, m_lo], 0)
        for q in range(4):
            products = []
            for c in range(2):
                hi, lo = split(rbuf[slot, c, :, q * rows : (q + 1) * rows])
                wide = dot(m_both, hi, 1, 0)
                products.append(wide[: 2 * focal] + wide[2 * focal :] + dot(m_hi, lo, 1, 0))
            p_t, q_t = products
            part[half, q, k] = jnp.concatenate([p_t[:focal] + q_t[focal:], p_t[focal:] - q_t[:focal]], 0)

        if half == 0:
            response_copy(w + SLOTS, slot).start()
        else:

            @pl.when(k < TILE - SLOTS)
            def _():
                response_copy(w + SLOTS, slot).start()

        return carry

    def core_sum(half):
        y_mine = rec // 2
        for yy in range(2):
            core_copy(half, yy).start()
        for yy in range(2):
            core_copy(half, yy).wait_recv()

        def add(k, carry):
            part[half, across, k] = part[half, across, k] + core_in[half, 1 - y_mine, k]
            return carry

        lax.fori_loop(0, TILE, add, 0)
        y_copy(half).start()

    def y_sum(half):
        y_mine = rec // 2
        y_copy(half).wait_recv()

        def add(k, carry):
            spread(
                g_buf, half, k, part[half, rec, k] + core_in[half, y_mine, k] + y_in[half, k]
            )
            return carry

        lax.fori_loop(0, TILE, add, 0)
        a2a_start(4 + half, half, g_buf, x2)

    for half in range(2):
        a2a_sent(half, half, g_buf, x1)
    for half in range(2):
        a2a_landed(2 + half, half, y_buf, fm)
        lax.fori_loop(0, TILE, functools.partial(h_step, half), 0)
        core_sum(half)
        if half == 1:
            y_sum(0)
            y_sum(1)
    a2a_sent(3, 1, y_buf, fm)
    for half in range(2):
        a2a_landed(4 + half, half, g_buf, x2)

    window(x2, y_buf)

    for half in range(2):
        a2a_start(6 + half, half, y_buf, upd)

    def final(half, k, carry):
        w = half * TILE + k
        value = collect(upd, half, k)
        for c in range(2):
            next_out[c, w] = direct[c, w] + value[c * focal : (c + 1) * focal]
        return carry

    for half in range(2):
        a2a_landed(6 + half, half, y_buf, upd)
        lax.fori_loop(0, TILE, functools.partial(final, half), 0)

    for half in range(2):
        a2a_sent(4 + half, half, g_buf, x2)
        a2a_sent(6 + half, half, y_buf, upd)
        ag_copy(1, half).wait_send()
        ag_copy(2, half).wait_send()
        y_copy(half).wait_send()
        for yy in range(2):
            core_copy(half, yy).wait_send()
    ag_copy(0, 1).wait_send()


def per_device_kernel(response, focus_plus, direct, onset):
    groups = lax.axis_size("freq")
    freq_dev, rows, positions = response.shape[1:]
    focal = focus_plus.shape[3]
    lane_parts = rows // 128
    into, back = cas_tables(groups)
    turned = (0, 1, 3, 2)
    out = jax.ShapeDtypeStruct((2, freq_dev, focal, rows), jnp.float32)
    traces = pltpu.VMEM((2, lane_parts, 2, groups, TILE * TILE, 128), jnp.float32)
    vmem = pl.BlockSpec(memory_space=pltpu.VMEM)
    anywhere = pl.BlockSpec(memory_space=pl.ANY)
    dma = pltpu.SemaphoreType.DMA
    minus, following = pl.pallas_call(
        functools.partial(kernel, groups),
        out_shape=(out, out),
        in_specs=[anywhere, anywhere, vmem, vmem, vmem, vmem],
        out_specs=(vmem, vmem),
        scratch_shapes=[
            pltpu.VMEM((4, 2, freq_dev, focal, rows), jnp.float32),
            pltpu.VMEM((SLOTS, 2, rows, positions), jnp.float32),
            traces, traces, traces, traces,
            pltpu.VMEM((2, 4, TILE, 2 * focal, rows), jnp.float32),
            pltpu.VMEM((2, 2, TILE, 2 * focal, rows), jnp.float32),
            pltpu.VMEM((2, TILE, 2 * focal, rows), jnp.float32),
            traces, traces,
            dma((3, 2)), dma((3, 2)), dma, dma((SLOTS,)),
            dma((8, groups)), dma((8, groups)),
            dma((2, 2)), dma((2, 2)), dma((2,)), dma((2,)),
        ],
        compiler_params=pltpu.CompilerParams(
            collective_id=0, has_side_effects=True, vmem_limit_bytes=61 * 1024 * 1024
        ),
    )(
        response,
        jnp.transpose(focus_plus, turned),
        jnp.transpose(direct, turned),
        onset.T.reshape(groups, TILE, rows),
        jnp.asarray(into),
        jnp.asarray(back),
    )
    return jnp.transpose(minus, turned), jnp.transpose(following, turned)


def per_device(response, focus_plus, direct, onset):
    freq_dev, rows, positions = response.shape[1:]
    fits = (
        lax.axis_size("rec") == 4
        and positions == 4 * rows
        and rows % 128 == 0
        and freq_dev == 2 * TILE
        and focus_plus.shape[3] == TILE * lax.axis_size("freq")
    )
    form = per_device_kernel if fits else per_device_general
    return form(response, focus_plus, direct, onset)


def solution(mesh):
    placed = (
        P(None, "freq", "rec", None),
        P(None, "freq", "rec", None),
        P(None, "freq", "rec", None),
        P("rec", None),
    )
    return jax.shard_map(
        per_device,
        mesh=mesh,
        in_specs=placed,
        out_specs=(P(None, "freq", "rec", None), P(None, "freq", "rec", None)),
        check_vma=False,
    )
```

```python
import functools
import math

import jax
import jax.numpy as jnp
import ml_dtypes
import numpy as np
from jax import lax
from jax.experimental import pallas as pl
from jax.experimental.pallas import tpu as pltpu
from jax.sharding import PartitionSpec as P

MESH = pl.DeviceIdType.MESH
SLOTS = 4
GROUP = 8
PARTS = 4
PART = 4
PAIR = 2


def full_einsum(form, left, right):
    return jnp.einsum(form, left, right, precision=lax.Precision.HIGHEST)


def make_tables(freq_total):
    counter = jnp.arange(freq_total, dtype=jnp.int32)
    phase_steps = counter[:, None] * counter[None, :] % freq_total
    phase_angle = phase_steps.astype(jnp.float32) * (2.0 * math.pi / freq_total)
    cosine = jnp.cos(phase_angle)
    sine_table = jnp.sin(phase_angle)
    inverse = (
        jnp.concatenate(
            [jnp.concatenate([cosine, -sine_table], 1), jnp.concatenate([sine_table, cosine], 1)], 0
        )
        / freq_total
    )
    forward = jnp.concatenate(
        [jnp.concatenate([cosine, sine_table], 1), jnp.concatenate([-sine_table, cosine], 1)], 0
    )
    return (inverse, forward)


def windowed(traces, onset_flat, inverse, forward):
    freq_total = traces.shape[1]
    stacked = traces.reshape(2 * freq_total, -1)
    time_traces = jnp.dot(inverse, stacked, precision=lax.Precision.HIGHEST)
    counter = jnp.arange(freq_total, dtype=jnp.int32)
    distance = jnp.minimum(counter, freq_total - counter)
    window_mask = (distance[:, None] < onset_flat[None, :]).astype(jnp.float32)
    window_mask = jnp.concatenate([window_mask, window_mask], 0)
    spectra = jnp.dot(forward, time_traces * window_mask, precision=lax.Precision.HIGHEST)
    return spectra.reshape(traces.shape)


def per_device_general(response, focus_plus, direct, onset):
    freq_dev = response.shape[1]
    row_count = response.shape[2]
    focal_count = focus_plus.shape[3]
    groups = lax.axis_size("freq")
    freq_index = lax.axis_index("freq")
    flat_count = row_count * focal_count
    piece_len = flat_count // groups
    local_onset = lax.dynamic_slice_in_dim(onset.reshape(-1), freq_index * piece_len, piece_len, 0)
    inverse, forward = make_tables(freq_dev * groups)
    shard_piece = lax.all_gather(focus_plus, "rec", axis=2, tiled=True)
    joined = jnp.concatenate([shard_piece[0], shard_piece[1]], axis=2)
    from_real = full_einsum("wrs,wsf->wrf", response[0], joined)
    from_imag = full_einsum("wrs,wsf->wrf", response[1], joined)
    new_real = from_real[:, :, :focal_count] - from_imag[:, :, focal_count:]
    new_imag = from_real[:, :, focal_count:] + from_imag[:, :, :focal_count]
    spectra = jnp.stack([new_real, new_imag]).reshape(2, freq_dev, flat_count)
    in_time = lax.all_to_all(spectra, "freq", split_axis=2, concat_axis=1, tiled=True)
    filtered = windowed(in_time, local_onset, inverse, forward)
    focus_minus = lax.all_to_all(filtered, "freq", split_axis=1, concat_axis=2, tiled=True).reshape(
        2, freq_dev, row_count, focal_count
    )
    minus_joined = jnp.concatenate([focus_minus[0], focus_minus[1]], axis=2)
    from_real = full_einsum("wrs,wrf->swf", response[0], minus_joined)
    from_imag = full_einsum("wrs,wrf->swf", response[1], minus_joined)
    h_real = from_real[:, :, :focal_count] + from_imag[:, :, focal_count:]
    h_imag = from_real[:, :, focal_count:] - from_imag[:, :, :focal_count]
    summed = lax.psum_scatter(
        jnp.stack([h_real, h_imag], axis=1), "rec", scatter_dimension=0, tiled=True
    )
    arranged_sum = jnp.transpose(summed, (1, 2, 0, 3)).reshape(2, freq_dev, flat_count)
    arranged = lax.all_to_all(arranged_sum, "freq", split_axis=2, concat_axis=1, tiled=True)
    windowed_back = windowed(arranged, local_onset, inverse, forward)
    returned = lax.all_to_all(
        windowed_back, "freq", split_axis=1, concat_axis=2, tiled=True
    ).reshape(2, freq_dev, row_count, focal_count)
    return (focus_minus, direct + returned)


def cas_tables(groups):
    per = PARTS * PART
    total = per * groups
    freq = np.array(
        [
            (f, g * per + q * PART + k)
            for q in range(PARTS) for g in range(groups) for f in range(PAIR) for k in range(PART)
        ]
    )
    time = np.array([(f, t) for f in range(PAIR) for t in range(total)])
    angle = time[:, None, 1] * freq[None, :, 1] % total * (2.0 * math.pi / total)
    into = np.where(time[:, None, 0] == freq[None, :, 0], np.cos(angle) + np.sin(angle), 0.0)

    def table(matrix):
        hi = matrix.astype(ml_dtypes.bfloat16)
        lo = (matrix - hi.astype(np.float64)).astype(ml_dtypes.bfloat16)
        return np.concatenate([hi, lo], 0)

    return table(into), table(into.T / total)


def split(value):
    hi = value.astype(jnp.bfloat16)
    lo = (value - hi.astype(jnp.float32)).astype(jnp.bfloat16)
    return hi, lo


def dot(left, right, left_dim, right_dim):
    return lax.dot_general(
        left, right, (((left_dim,), (right_dim,)), ((), ())), preferred_element_type=jnp.float32
    )


def kernel(
    groups,
    resp, plus, direct, onset, into, back,
    minus_out, next_out,
    gathered, rbuf, g_buf, x1, y_buf, fm, part, core_in, y_in, x2, upd,
    ag_s, ag_r, own_sem, r_sem, a_s, a_r, rc_s, rc_r, ry_s, ry_r,
):
    me = lax.axis_index("freq")
    rec = lax.axis_index("rec")
    core = lax.rem(rec, 2)
    sibling = rec + 1 - 2 * core
    across = lax.rem(rec + 2, 4)
    diagonal = lax.rem(sibling + 2, 4)
    rows = resp.shape[2]
    lane_parts = rows // 128
    focal = plus.shape[2]
    total = PARTS * PART * groups

    barrier = pltpu.get_barrier_semaphore()
    for d in range(1, groups):
        pl.semaphore_signal(
            barrier, inc=1, device_id=(lax.rem(me + d, groups), rec), device_id_type=MESH
        )
    for other in (sibling, across):
        pl.semaphore_signal(barrier, inc=1, device_id=(me, other), device_id_type=MESH)

    def response_copy(w, slot):
        return pltpu.make_async_copy(resp.at[:, w], rbuf.at[slot], r_sem.at[slot])

    for k in range(SLOTS):
        response_copy(k, k).start()
    pl.semaphore_wait(barrier, groups + 1)

    def remote(src, dst, s_sem, d_sem, to):
        return pltpu.make_async_remote_copy(
            src_ref=src, dst_ref=dst, send_sem=s_sem, recv_sem=d_sem, device_id=to, device_id_type=MESH
        )

    def ag_copy(kind, half):
        span = pl.ds(half * PART, PART)
        if kind == 2:
            return remote(
                gathered.at[across, :, span], gathered.at[across, :, span],
                ag_s.at[2, half], ag_r.at[2, half], (me, sibling),
            )
        return remote(
            plus.at[:, span], gathered.at[rec, :, span],
            ag_s.at[kind, half], ag_r.at[kind, half], (me, (across, sibling)[kind]),
        )

    def ag_landed(kind, half):
        span = pl.ds(half * PART, PART)
        slot = (across, sibling, diagonal)[kind]
        place = gathered.at[slot, :, span]
        return remote(
            place, place, ag_s.at[kind, half], ag_r.at[kind, half], (me, (across, sibling, sibling)[kind])
        )

    def a2a_peers(phase, src, dst, pick):
        return [
            remote(pick(src, peer), pick(dst, me), a_s.at[phase, d], a_r.at[phase, d], (peer, rec))
            for d in range(1, groups)
            for peer in (lax.rem(me + d, groups),)
        ]

    def a2a_begin(phase, src, dst, pick):
        for copy in a2a_peers(phase, src, dst, pick):
            copy.start()
        pltpu.make_async_copy(pick(src, me), pick(dst, me), a_r.at[phase, 0]).start()

    def a2a_left(phase, src, dst, pick):
        for copy in a2a_peers(phase, src, dst, pick):
            copy.wait_send()

    def a2a_arrived(phase, src, dst, pick):
        pltpu.make_async_copy(pick(src, me), pick(dst, me), a_r.at[phase, 0]).wait()
        for d in range(1, groups):
            peer = lax.rem(me + groups - d, groups)
            place = pick(dst, peer)
            remote(place, place, a_s.at[phase, d], a_r.at[phase, d], (peer, rec)).wait_recv()

    def of_part(q):
        return lambda ref, place: ref.at[q, :, :, place]

    def of_real(c):
        return lambda ref, place: ref.at[:, :, c, place]

    def a2a_start(phase, q, src, dst):
        a2a_begin(phase, src, dst, of_part(q))

    def a2a_sent(phase, q, src, dst):
        a2a_left(phase, src, dst, of_part(q))

    def a2a_landed(phase, q, src, dst):
        a2a_arrived(phase, src, dst, of_part(q))

    def last_start(c):
        a2a_begin(3 * PARTS + c, y_buf, upd, of_real(c))

    def last_sent(c):
        a2a_left(3 * PARTS + c, y_buf, upd, of_real(c))

    def last_landed(c):
        a2a_arrived(3 * PARTS + c, y_buf, upd, of_real(c))

    def spread(dst, half, k, value):
        for lh in range(lane_parts):
            for c in range(2):
                for grp in range(groups):
                    at = (c * groups + grp) * GROUP
                    dst[half, lh, c, grp, pl.ds(k, GROUP, stride=PART), :] = value[
                        at : at + GROUP, lh * 128 : (lh + 1) * 128
                    ]

    def window(src, dst, c):
        row = lax.broadcasted_iota(jnp.int32, (PAIR * total, rows), 0)
        time = lax.rem(row, total)
        distance = jnp.minimum(time, total - time)
        tall = groups * PAIR * PART

        def one(f, carry):
            span = pl.ds(pl.multiple_of(f * PAIR * PART, PAIR * PART), PAIR * PART)
            first = onset[me, pl.ds(PAIR * f, 1), :]
            second = onset[me, pl.ds(PAIR * f + 1, 1), :]
            keep = distance < jnp.where(row < total, first, second)
            block = jnp.concatenate(
                [
                    jnp.concatenate(
                        [src[q, lh, c, :, span, :].reshape(tall, 128) for q in range(PARTS)], 0
                    )
                    for lh in range(lane_parts)
                ],
                1,
            )
            for step in range(2):
                hi, lo = split(block)
                table = (into, back)[step]
                both = dot(table[...], hi, 1, 0)
                block = both[: PAIR * total] + both[PAIR * total :] + dot(table[: PAIR * total], lo, 1, 0)
                if step == 0:
                    block = jnp.where(keep, block, 0.0)
            for q in range(PARTS):
                for lh in range(lane_parts):
                    dst[q, lh, c, :, span, :] = block[
                        q * tall : (q + 1) * tall, lh * 128 : (lh + 1) * 128
                    ].reshape(groups, PAIR * PART, 128)
            return carry

        lax.fori_loop(0, GROUP // PAIR, one, 0)

    own = pltpu.make_async_copy(plus, gathered.at[rec], own_sem)
    ag_copy(0, 0).start()
    own.start()
    for part_no in range(PARTS):
        ag_copy(1, part_no).start()
    own.wait()

    def g_step(half, k, carry):
        w = half * PART + k
        slot = lax.rem(w, SLOTS)
        response_copy(w, slot).wait()
        plus_t = jnp.concatenate(
            [jnp.concatenate([gathered[q, c, w] for q in range(4)], 1) for c in range(2)], 0
        )
        f_hi, f_lo = split(plus_t)
        f_both = jnp.concatenate([f_hi, f_lo], 0)
        products = []
        for c in range(2):
            hi, lo = split(rbuf[slot, c])
            wide = dot(hi, f_both, 1, 1)
            products.append(wide[:, : 2 * focal] + wide[:, 2 * focal :] + dot(lo, f_hi, 1, 1))
        p_t, q_t = products[0].T, products[1].T
        spread(g_buf, half, k, jnp.concatenate([p_t[:focal] - q_t[focal:], p_t[focal:] + q_t[:focal]], 0))
        response_copy(lax.rem(w + SLOTS, PARTS * PART), slot).start()
        return carry

    for half in range(PARTS):
        ag_landed(0, half).wait_recv()
        if half == 0:
            ag_copy(0, 0).wait_send()
            ag_copy(0, 1).start()
        if half + 2 < PARTS:
            ag_copy(0, half + 2).start()
        ag_copy(2, half).start()
        ag_landed(1, half).wait_recv()
        ag_landed(2, half).wait_recv()
        lax.fori_loop(0, PART, functools.partial(g_step, half), 0)
        a2a_start(half, half, g_buf, x1)
    for half in range(PARTS):
        a2a_landed(half, half, g_buf, x1)

    window(x1, y_buf, 0)
    window(x1, y_buf, 1)

    a2a_start(PARTS, 0, y_buf, fm)
    a2a_start(PARTS + 1, 1, y_buf, fm)

    def core_copy(half, yy):
        return remote(
            part.at[half, 2 * yy + 1 - core], core_in.at[half, yy],
            rc_s.at[half, yy], rc_r.at[half, yy], (me, sibling),
        )

    def y_copy(half):
        return remote(
            part.at[half, across], y_in.at[half], ry_s.at[half], ry_r.at[half], (me, across)
        )

    def collect(src, half, k, parts):
        return jnp.concatenate(
            [
                jnp.concatenate(
                    [
                        src[half, lh, c, grp, pl.ds(k, GROUP, stride=PART), :]
                        for c in parts
                        for grp in range(groups)
                    ],
                    0,
                )
                for lh in range(lane_parts)
            ],
            1,
        )

    def h_step(half, k, carry):
        w = half * PART + k
        slot = lax.rem(w, SLOTS)
        minus_t = collect(fm, half, k, (0, 1))
        for c in range(2):
            minus_out[c, w] = minus_t[c * focal : (c + 1) * focal]
        response_copy(w, slot).wait()
        m_hi, m_lo = split(minus_t)
        m_both = jnp.concatenate([m_hi, m_lo], 0)
        for q in range(4):
            products = []
            for c in range(2):
                hi, lo = split(rbuf[slot, c, :, q * rows : (q + 1) * rows])
                wide = dot(m_both, hi, 1, 0)
                products.append(wide[: 2 * focal] + wide[2 * focal :] + dot(m_hi, lo, 1, 0))
            p_t, q_t = products
            part[half, q, k] = jnp.concatenate([p_t[:focal] + q_t[focal:], p_t[focal:] - q_t[:focal]], 0)

        @pl.when(w + SLOTS < PARTS * PART)
        def _():
            response_copy(w + SLOTS, slot).start()

        return carry

    def core_sum(half):
        y_mine = rec // 2
        for yy in range(2):
            core_copy(half, yy).start()
        for yy in range(2):
            core_copy(half, yy).wait_recv()

        def add(k, carry):
            part[half, across, k] = part[half, across, k] + core_in[half, 1 - y_mine, k]
            return carry

        lax.fori_loop(0, PART, add, 0)
        y_copy(half).start()

    def y_sum(half):
        y_mine = rec // 2
        y_copy(half).wait_recv()

        def add(k, carry):
            spread(
                g_buf, half, k, part[half, rec, k] + core_in[half, y_mine, k] + y_in[half, k]
            )
            return carry

        lax.fori_loop(0, PART, add, 0)
        a2a_start(2 * PARTS + half, half, g_buf, x2)

    for half in range(PARTS):
        a2a_sent(half, half, g_buf, x1)
    for half in range(PARTS):
        if half + 2 < PARTS:
            a2a_sent(PARTS + half, half, y_buf, fm)
            a2a_start(PARTS + half + 2, half + 2, y_buf, fm)
        a2a_landed(PARTS + half, half, y_buf, fm)
        lax.fori_loop(0, PART, functools.partial(h_step, half), 0)
        core_sum(half)
        if half > 0:
            y_sum(half - 1)
    y_sum(PARTS - 1)
    for half in range(PARTS - 2, PARTS):
        a2a_sent(PARTS + half, half, y_buf, fm)
    for half in range(PARTS):
        a2a_landed(2 * PARTS + half, half, g_buf, x2)

    for c in range(2):
        window(x2, y_buf, c)
        last_start(c)

    def final(c, w, carry):
        value = collect(upd, w // PART, lax.rem(w, PART), (c,))
        next_out[c, w] = direct[c, w] + value
        return carry

    for c in range(2):
        last_landed(c)
        lax.fori_loop(0, PARTS * PART, functools.partial(final, c), 0)

    for c in range(2):
        last_sent(c)
    for half in range(PARTS):
        a2a_sent(2 * PARTS + half, half, g_buf, x2)
        if half > 0:
            ag_copy(0, half).wait_send()
        ag_copy(1, half).wait_send()
        ag_copy(2, half).wait_send()
        y_copy(half).wait_send()
        for yy in range(2):
            core_copy(half, yy).wait_send()


def per_device_kernel(response, focus_plus, direct, onset):
    groups = lax.axis_size("freq")
    freq_dev, rows, positions = response.shape[1:]
    focal = focus_plus.shape[3]
    lane_parts = rows // 128
    into, back = cas_tables(groups)
    turned = (0, 1, 3, 2)
    out = jax.ShapeDtypeStruct((2, freq_dev, focal, rows), jnp.float32)
    traces = pltpu.VMEM((PARTS, lane_parts, 2, groups, GROUP * PART, 128), jnp.float32)
    vmem = pl.BlockSpec(memory_space=pltpu.VMEM)
    anywhere = pl.BlockSpec(memory_space=pl.ANY)
    dma = pltpu.SemaphoreType.DMA
    minus, following = pl.pallas_call(
        functools.partial(kernel, groups),
        out_shape=(out, out),
        in_specs=[anywhere, anywhere, vmem, vmem, vmem, vmem],
        out_specs=(vmem, vmem),
        scratch_shapes=[
            pltpu.VMEM((4, 2, freq_dev, focal, rows), jnp.float32),
            pltpu.VMEM((SLOTS, 2, rows, positions), jnp.float32),
            traces, traces, traces, traces,
            pltpu.VMEM((PARTS, 4, PART, 2 * focal, rows), jnp.float32),
            pltpu.VMEM((PARTS, 2, PART, 2 * focal, rows), jnp.float32),
            pltpu.VMEM((PARTS, PART, 2 * focal, rows), jnp.float32),
            traces, traces,
            dma((3, PARTS)), dma((3, PARTS)), dma, dma((SLOTS,)),
            dma((3 * PARTS + 2, groups)), dma((3 * PARTS + 2, groups)),
            dma((PARTS, 2)), dma((PARTS, 2)), dma((PARTS,)), dma((PARTS,)),
        ],
        compiler_params=pltpu.CompilerParams(
            collective_id=0, has_side_effects=True, vmem_limit_bytes=61 * 1024 * 1024
        ),
    )(
        response,
        jnp.transpose(focus_plus, turned),
        jnp.transpose(direct, turned),
        onset.T.reshape(groups, GROUP, rows),
        jnp.asarray(into),
        jnp.asarray(back),
    )
    return jnp.transpose(minus, turned), jnp.transpose(following, turned)


def per_device(response, focus_plus, direct, onset):
    freq_dev, rows, positions = response.shape[1:]
    fits = (
        lax.axis_size("rec") == 4
        and positions == 4 * rows
        and rows % 128 == 0
        and freq_dev == PARTS * PART
        and focus_plus.shape[3] == GROUP * lax.axis_size("freq")
    )
    form = per_device_kernel if fits else per_device_general
    return form(response, focus_plus, direct, onset)


def solution(mesh):
    placed = (
        P(None, "freq", "rec", None),
        P(None, "freq", "rec", None),
        P(None, "freq", "rec", None),
        P("rec", None),
    )
    return jax.shard_map(
        per_device,
        mesh=mesh,
        in_specs=placed,
        out_specs=(P(None, "freq", "rec", None), P(None, "freq", "rec", None)),
        check_vma=False,
    )
```

```python
import functools
import math

import jax
import jax.numpy as jnp
import ml_dtypes
import numpy as np
from jax import lax
from jax.experimental import pallas as pl
from jax.experimental.pallas import tpu as pltpu
from jax.sharding import PartitionSpec as P

MESH = pl.DeviceIdType.MESH
SLOTS = 4
GROUP = 8
PARTS = 4
PART = 4
PAIR = 2


def full_einsum(form, left, right):
    return jnp.einsum(form, left, right, precision=lax.Precision.HIGHEST)


def make_tables(freq_total):
    counter = jnp.arange(freq_total, dtype=jnp.int32)
    phase_steps = counter[:, None] * counter[None, :] % freq_total
    phase_angle = phase_steps.astype(jnp.float32) * (2.0 * math.pi / freq_total)
    cosine = jnp.cos(phase_angle)
    sine_table = jnp.sin(phase_angle)
    inverse = (
        jnp.concatenate(
            [jnp.concatenate([cosine, -sine_table], 1), jnp.concatenate([sine_table, cosine], 1)], 0
        )
        / freq_total
    )
    forward = jnp.concatenate(
        [jnp.concatenate([cosine, sine_table], 1), jnp.concatenate([-sine_table, cosine], 1)], 0
    )
    return (inverse, forward)


def windowed(traces, onset_flat, inverse, forward):
    freq_total = traces.shape[1]
    stacked = traces.reshape(2 * freq_total, -1)
    time_traces = jnp.dot(inverse, stacked, precision=lax.Precision.HIGHEST)
    counter = jnp.arange(freq_total, dtype=jnp.int32)
    distance = jnp.minimum(counter, freq_total - counter)
    window_mask = (distance[:, None] < onset_flat[None, :]).astype(jnp.float32)
    window_mask = jnp.concatenate([window_mask, window_mask], 0)
    spectra = jnp.dot(forward, time_traces * window_mask, precision=lax.Precision.HIGHEST)
    return spectra.reshape(traces.shape)


def per_device_general(response, focus_plus, direct, onset):
    freq_dev = response.shape[1]
    row_count = response.shape[2]
    focal_count = focus_plus.shape[3]
    groups = lax.axis_size("freq")
    freq_index = lax.axis_index("freq")
    flat_count = row_count * focal_count
    piece_len = flat_count // groups
    local_onset = lax.dynamic_slice_in_dim(onset.reshape(-1), freq_index * piece_len, piece_len, 0)
    inverse, forward = make_tables(freq_dev * groups)
    shard_piece = lax.all_gather(focus_plus, "rec", axis=2, tiled=True)
    joined = jnp.concatenate([shard_piece[0], shard_piece[1]], axis=2)
    from_real = full_einsum("wrs,wsf->wrf", response[0], joined)
    from_imag = full_einsum("wrs,wsf->wrf", response[1], joined)
    new_real = from_real[:, :, :focal_count] - from_imag[:, :, focal_count:]
    new_imag = from_real[:, :, focal_count:] + from_imag[:, :, :focal_count]
    spectra = jnp.stack([new_real, new_imag]).reshape(2, freq_dev, flat_count)
    in_time = lax.all_to_all(spectra, "freq", split_axis=2, concat_axis=1, tiled=True)
    filtered = windowed(in_time, local_onset, inverse, forward)
    focus_minus = lax.all_to_all(filtered, "freq", split_axis=1, concat_axis=2, tiled=True).reshape(
        2, freq_dev, row_count, focal_count
    )
    minus_joined = jnp.concatenate([focus_minus[0], focus_minus[1]], axis=2)
    from_real = full_einsum("wrs,wrf->swf", response[0], minus_joined)
    from_imag = full_einsum("wrs,wrf->swf", response[1], minus_joined)
    h_real = from_real[:, :, :focal_count] + from_imag[:, :, focal_count:]
    h_imag = from_real[:, :, focal_count:] - from_imag[:, :, :focal_count]
    summed = lax.psum_scatter(
        jnp.stack([h_real, h_imag], axis=1), "rec", scatter_dimension=0, tiled=True
    )
    arranged_sum = jnp.transpose(summed, (1, 2, 0, 3)).reshape(2, freq_dev, flat_count)
    arranged = lax.all_to_all(arranged_sum, "freq", split_axis=2, concat_axis=1, tiled=True)
    windowed_back = windowed(arranged, local_onset, inverse, forward)
    returned = lax.all_to_all(
        windowed_back, "freq", split_axis=1, concat_axis=2, tiled=True
    ).reshape(2, freq_dev, row_count, focal_count)
    return (focus_minus, direct + returned)


def cas_tables(groups):
    per = PARTS * PART
    total = per * groups
    freq = np.array(
        [
            (f, g * per + q * PART + k)
            for q in range(PARTS) for g in range(groups) for f in range(PAIR) for k in range(PART)
        ]
    )
    time = np.array([(f, t) for f in range(PAIR) for t in range(total)])
    angle = time[:, None, 1] * freq[None, :, 1] % total * (2.0 * math.pi / total)
    into = np.where(time[:, None, 0] == freq[None, :, 0], np.cos(angle) + np.sin(angle), 0.0)

    def table(matrix):
        hi = matrix.astype(ml_dtypes.bfloat16)
        lo = (matrix - hi.astype(np.float64)).astype(ml_dtypes.bfloat16)
        return np.concatenate([hi, lo], 0)

    return table(into), table(into.T / total)


def split(value):
    hi = value.astype(jnp.bfloat16)
    lo = (value - hi.astype(jnp.float32)).astype(jnp.bfloat16)
    return hi, lo


def dot(left, right, left_dim, right_dim):
    return lax.dot_general(
        left, right, (((left_dim,), (right_dim,)), ((), ())), preferred_element_type=jnp.float32
    )


def kernel(
    groups,
    resp, plus, direct, onset, into, back,
    minus_out, next_out,
    gathered, rbuf, g_buf, x1, y_buf, fm, part, core_in, y_in, x2, upd,
    ag_s, ag_r, own_sem, r_sem, a_s, a_r, rc_s, rc_r, ry_s, ry_r,
):
    me = lax.axis_index("freq")
    rec = lax.axis_index("rec")
    core = lax.rem(rec, 2)
    sibling = rec + 1 - 2 * core
    across = lax.rem(rec + 2, 4)
    diagonal = lax.rem(sibling + 2, 4)
    rows = resp.shape[2]
    lane_parts = rows // 128
    focal = plus.shape[2]
    total = PARTS * PART * groups

    barrier = pltpu.get_barrier_semaphore()
    for d in range(1, groups):
        pl.semaphore_signal(
            barrier, inc=1, device_id=(lax.rem(me + d, groups), rec), device_id_type=MESH
        )
    for other in (sibling, across):
        pl.semaphore_signal(barrier, inc=1, device_id=(me, other), device_id_type=MESH)

    def response_copy(w, slot):
        return pltpu.make_async_copy(resp.at[:, w], rbuf.at[slot], r_sem.at[slot])

    for k in range(SLOTS):
        response_copy(k, k).start()
    pl.semaphore_wait(barrier, groups + 1)

    def remote(src, dst, s_sem, d_sem, to):
        return pltpu.make_async_remote_copy(
            src_ref=src, dst_ref=dst, send_sem=s_sem, recv_sem=d_sem, device_id=to, device_id_type=MESH
        )

    def ag_copy(kind, half):
        span = pl.ds(half * PART, PART)
        if kind == 2:
            return remote(
                gathered.at[across, :, span], gathered.at[across, :, span],
                ag_s.at[2, half], ag_r.at[2, half], (me, sibling),
            )
        return remote(
            plus.at[:, span], gathered.at[rec, :, span],
            ag_s.at[kind, half], ag_r.at[kind, half], (me, (across, sibling)[kind]),
        )

    def ag_landed(kind, half):
        span = pl.ds(half * PART, PART)
        slot = (across, sibling, diagonal)[kind]
        place = gathered.at[slot, :, span]
        return remote(
            place, place, ag_s.at[kind, half], ag_r.at[kind, half], (me, (across, sibling, sibling)[kind])
        )

    def a2a_peers(phase, src, dst, pick):
        return [
            remote(pick(src, peer), pick(dst, me), a_s.at[phase, d], a_r.at[phase, d], (peer, rec))
            for d in sorted(range(1, groups), key=lambda d: -abs(2 * d - groups))
            for peer in (lax.rem(me + d, groups),)
        ]

    def a2a_begin(phase, src, dst, pick):
        for copy in a2a_peers(phase, src, dst, pick):
            copy.start()
        pltpu.make_async_copy(pick(src, me), pick(dst, me), a_r.at[phase, 0]).start()

    def a2a_left(phase, src, dst, pick):
        for copy in a2a_peers(phase, src, dst, pick):
            copy.wait_send()

    def a2a_arrived(phase, src, dst, pick):
        pltpu.make_async_copy(pick(src, me), pick(dst, me), a_r.at[phase, 0]).wait()
        for d in range(1, groups):
            peer = lax.rem(me + groups - d, groups)
            place = pick(dst, peer)
            remote(place, place, a_s.at[phase, d], a_r.at[phase, d], (peer, rec)).wait_recv()

    def of_part(q):
        return lambda ref, place: ref.at[q, :, :, place]

    def of_real(c):
        return lambda ref, place: ref.at[:, :, c, place]

    def a2a_start(phase, q, src, dst):
        a2a_begin(phase, src, dst, of_part(q))

    def a2a_sent(phase, q, src, dst):
        a2a_left(phase, src, dst, of_part(q))

    def a2a_landed(phase, q, src, dst):
        a2a_arrived(phase, src, dst, of_part(q))

    def last_start(c):
        a2a_begin(3 * PARTS + c, y_buf, upd, of_real(c))

    def last_sent(c):
        a2a_left(3 * PARTS + c, y_buf, upd, of_real(c))

    def last_landed(c):
        a2a_arrived(3 * PARTS + c, y_buf, upd, of_real(c))

    def spread(dst, half, k, value):
        for lh in range(lane_parts):
            for c in range(2):
                for grp in range(groups):
                    at = (c * groups + grp) * GROUP
                    dst[half, lh, c, grp, pl.ds(k, GROUP, stride=PART), :] = value[
                        at : at + GROUP, lh * 128 : (lh + 1) * 128
                    ]

    def window(src, dst, c):
        row = lax.broadcasted_iota(jnp.int32, (PAIR * total, rows), 0)
        time = lax.rem(row, total)
        distance = jnp.minimum(time, total - time)
        tall = groups * PAIR * PART

        def one(f, carry):
            span = pl.ds(pl.multiple_of(f * PAIR * PART, PAIR * PART), PAIR * PART)
            first = onset[me, pl.ds(PAIR * f, 1), :]
            second = onset[me, pl.ds(PAIR * f + 1, 1), :]
            keep = distance < jnp.where(row < total, first, second)
            block = jnp.concatenate(
                [
                    jnp.concatenate(
                        [src[q, lh, c, :, span, :].reshape(tall, 128) for q in range(PARTS)], 0
                    )
                    for lh in range(lane_parts)
                ],
                1,
            )
            for step in range(2):
                hi, lo = split(block)
                table = (into, back)[step]
                both = dot(table[...], hi, 1, 0)
                block = both[: PAIR * total] + both[PAIR * total :] + dot(table[: PAIR * total], lo, 1, 0)
                if step == 0:
                    block = jnp.where(keep, block, 0.0)
            for q in range(PARTS):
                for lh in range(lane_parts):
                    dst[q, lh, c, :, span, :] = block[
                        q * tall : (q + 1) * tall, lh * 128 : (lh + 1) * 128
                    ].reshape(groups, PAIR * PART, 128)
            return carry

        lax.fori_loop(0, GROUP // PAIR, one, 0)

    own = pltpu.make_async_copy(plus, gathered.at[rec], own_sem)
    ag_copy(0, 0).start()
    own.start()
    for part_no in range(PARTS):
        ag_copy(1, part_no).start()
    own.wait()

    def g_step(half, k, carry):
        w = half * PART + k
        slot = lax.rem(w, SLOTS)
        response_copy(w, slot).wait()
        plus_t = jnp.concatenate(
            [jnp.concatenate([gathered[q, c, w] for q in range(4)], 1) for c in range(2)], 0
        )
        f_hi, f_lo = split(plus_t)
        f_both = jnp.concatenate([f_hi, f_lo], 0)
        products = []
        for c in range(2):
            hi, lo = split(rbuf[slot, c])
            wide = dot(hi, f_both, 1, 1)
            products.append(wide[:, : 2 * focal] + wide[:, 2 * focal :] + dot(lo, f_hi, 1, 1))
        p_t, q_t = products[0].T, products[1].T
        spread(g_buf, half, k, jnp.concatenate([p_t[:focal] - q_t[focal:], p_t[focal:] + q_t[:focal]], 0))
        response_copy(lax.rem(w + SLOTS, PARTS * PART), slot).start()
        return carry

    for half in range(PARTS):
        ag_landed(0, half).wait_recv()
        if half == 0:
            ag_copy(0, 0).wait_send()
            ag_copy(0, 1).start()
        if half + 2 < PARTS:
            ag_copy(0, half + 2).start()
        ag_copy(2, half).start()
        ag_landed(1, half).wait_recv()
        ag_landed(2, half).wait_recv()
        lax.fori_loop(0, PART, functools.partial(g_step, half), 0)
        a2a_start(half, half, g_buf, x1)
    for half in range(PARTS):
        a2a_landed(half, half, g_buf, x1)

    window(x1, y_buf, 0)
    window(x1, y_buf, 1)

    a2a_start(PARTS, 0, y_buf, fm)
    a2a_start(PARTS + 1, 1, y_buf, fm)

    def core_copy(half, yy):
        return remote(
            part.at[half, 2 * yy + 1 - core], core_in.at[half, yy],
            rc_s.at[half, yy], rc_r.at[half, yy], (me, sibling),
        )

    def y_copy(half):
        return remote(
            part.at[half, across], y_in.at[half], ry_s.at[half], ry_r.at[half], (me, across)
        )

    def collect(src, half, k, parts):
        return jnp.concatenate(
            [
                jnp.concatenate(
                    [
                        src[half, lh, c, grp, pl.ds(k, GROUP, stride=PART), :]
                        for c in parts
                        for grp in range(groups)
                    ],
                    0,
                )
                for lh in range(lane_parts)
            ],
            1,
        )

    def h_step(half, k, carry):
        w = half * PART + k
        slot = lax.rem(w, SLOTS)
        minus_t = collect(fm, half, k, (0, 1))
        for c in range(2):
            minus_out[c, w] = minus_t[c * focal : (c + 1) * focal]
        response_copy(w, slot).wait()
        m_hi, m_lo = split(minus_t)
        m_both = jnp.concatenate([m_hi, m_lo], 0)
        for q in range(4):
            products = []
            for c in range(2):
                hi, lo = split(rbuf[slot, c, :, q * rows : (q + 1) * rows])
                wide = dot(m_both, hi, 1, 0)
                products.append(wide[: 2 * focal] + wide[2 * focal :] + dot(m_hi, lo, 1, 0))
            p_t, q_t = products
            part[half, q, k] = jnp.concatenate([p_t[:focal] + q_t[focal:], p_t[focal:] - q_t[:focal]], 0)

        @pl.when(w + SLOTS < PARTS * PART)
        def _():
            response_copy(w + SLOTS, slot).start()

        return carry

    def core_sum(half):
        y_mine = rec // 2
        for yy in range(2):
            core_copy(half, yy).start()
        for yy in range(2):
            core_copy(half, yy).wait_recv()

        def add(k, carry):
            part[half, across, k] = part[half, across, k] + core_in[half, 1 - y_mine, k]
            return carry

        lax.fori_loop(0, PART, add, 0)
        y_copy(half).start()

    def y_sum(half):
        y_mine = rec // 2
        y_copy(half).wait_recv()

        def add(k, carry):
            spread(
                g_buf, half, k, part[half, rec, k] + core_in[half, y_mine, k] + y_in[half, k]
            )
            return carry

        lax.fori_loop(0, PART, add, 0)
        a2a_start(2 * PARTS + half, half, g_buf, x2)

    for half in range(PARTS):
        a2a_sent(half, half, g_buf, x1)
    for half in range(PARTS):
        if half + 2 < PARTS:
            a2a_sent(PARTS + half, half, y_buf, fm)
            a2a_start(PARTS + half + 2, half + 2, y_buf, fm)
        a2a_landed(PARTS + half, half, y_buf, fm)
        lax.fori_loop(0, PART, functools.partial(h_step, half), 0)
        core_sum(half)
        if half > 0:
            y_sum(half - 1)
    y_sum(PARTS - 1)
    for half in range(PARTS - 2, PARTS):
        a2a_sent(PARTS + half, half, y_buf, fm)
    for half in range(PARTS):
        a2a_landed(2 * PARTS + half, half, g_buf, x2)

    for c in range(2):
        window(x2, y_buf, c)
        last_start(c)

    def final(c, w, carry):
        value = collect(upd, w // PART, lax.rem(w, PART), (c,))
        next_out[c, w] = direct[c, w] + value
        return carry

    for c in range(2):
        last_landed(c)
        lax.fori_loop(0, PARTS * PART, functools.partial(final, c), 0)

    for c in range(2):
        last_sent(c)
    for half in range(PARTS):
        a2a_sent(2 * PARTS + half, half, g_buf, x2)
        if half > 0:
            ag_copy(0, half).wait_send()
        ag_copy(1, half).wait_send()
        ag_copy(2, half).wait_send()
        y_copy(half).wait_send()
        for yy in range(2):
            core_copy(half, yy).wait_send()


def per_device_kernel(response, focus_plus, direct, onset):
    groups = lax.axis_size("freq")
    freq_dev, rows, positions = response.shape[1:]
    focal = focus_plus.shape[3]
    lane_parts = rows // 128
    into, back = cas_tables(groups)
    turned = (0, 1, 3, 2)
    out = jax.ShapeDtypeStruct((2, freq_dev, focal, rows), jnp.float32)
    traces = pltpu.VMEM((PARTS, lane_parts, 2, groups, GROUP * PART, 128), jnp.float32)
    vmem = pl.BlockSpec(memory_space=pltpu.VMEM)
    anywhere = pl.BlockSpec(memory_space=pl.ANY)
    dma = pltpu.SemaphoreType.DMA
    minus, following = pl.pallas_call(
        functools.partial(kernel, groups),
        out_shape=(out, out),
        in_specs=[anywhere, anywhere, vmem, vmem, vmem, vmem],
        out_specs=(vmem, vmem),
        scratch_shapes=[
            pltpu.VMEM((4, 2, freq_dev, focal, rows), jnp.float32),
            pltpu.VMEM((SLOTS, 2, rows, positions), jnp.float32),
            traces, traces, traces, traces,
            pltpu.VMEM((PARTS, 4, PART, 2 * focal, rows), jnp.float32),
            pltpu.VMEM((PARTS, 2, PART, 2 * focal, rows), jnp.float32),
            pltpu.VMEM((PARTS, PART, 2 * focal, rows), jnp.float32),
            traces, traces,
            dma((3, PARTS)), dma((3, PARTS)), dma, dma((SLOTS,)),
            dma((3 * PARTS + 2, groups)), dma((3 * PARTS + 2, groups)),
            dma((PARTS, 2)), dma((PARTS, 2)), dma((PARTS,)), dma((PARTS,)),
        ],
        compiler_params=pltpu.CompilerParams(
            collective_id=0, has_side_effects=True, vmem_limit_bytes=61 * 1024 * 1024
        ),
    )(
        response,
        jnp.transpose(focus_plus, turned),
        jnp.transpose(direct, turned),
        onset.T.reshape(groups, GROUP, rows),
        jnp.asarray(into),
        jnp.asarray(back),
    )
    return jnp.transpose(minus, turned), jnp.transpose(following, turned)


def per_device(response, focus_plus, direct, onset):
    freq_dev, rows, positions = response.shape[1:]
    fits = (
        lax.axis_size("rec") == 4
        and positions == 4 * rows
        and rows % 128 == 0
        and freq_dev == PARTS * PART
        and focus_plus.shape[3] == GROUP * lax.axis_size("freq")
    )
    form = per_device_kernel if fits else per_device_general
    return form(response, focus_plus, direct, onset)


def solution(mesh):
    placed = (
        P(None, "freq", "rec", None),
        P(None, "freq", "rec", None),
        P(None, "freq", "rec", None),
        P("rec", None),
    )
    return jax.shard_map(
        per_device,
        mesh=mesh,
        in_specs=placed,
        out_specs=(P(None, "freq", "rec", None), P(None, "freq", "rec", None)),
        check_vma=False,
    )
```
